32 devices in a mesh: shot: 8 (over z, x), depth: 4 (over y, core).
Axes of the slice: x: 2, y: 2, z: 4, core: 2. Of those that a mesh axis runs over, the one named last changes fastest.
Arguments:
- prev_fields: float32 [8, 2, 32, 16, 128], P('shot', None, 'depth'), may hold values from -6 to 6
- cur_fields: float32 [8, 2, 32, 16, 128], P('shot', None, 'depth'), may hold values from -6 to 6
- speed_term: bfloat16 [8, 32, 16, 128], P('shot', 'depth'), may hold values from 0.039794922 to 0.119628906
- epsilon: bfloat16 [8, 32, 16, 128], P('shot', 'depth'), may hold values from 0 to 0.25
- tilt: bfloat16 [8, 32, 16, 128], P('shot', 'depth'), may hold values from 0 to 1.5
- azimuth: bfloat16 [8, 32, 16, 128], P('shot', 'depth'), may hold values from -3.140625 to 3.140625
- aperture_anchor: int32 [8], replicated, may hold values from -8 to 24
- slot_block: int32 [32], replicated, may hold values from 0 to 31, as said below
- band_width: int32 [32], replicated, may hold values from 1 to 4
- depth_damp: float32 [32], replicated, may hold values from 0.02 to 0.1
Outputs:
- gradient: float32 [32, 128, 32], P('shot', 'depth')
The draws below stay inside these ranges and needn't reach their ends.
Inputs may be any that keep to these rules, and one draw needn't show every extreme that they name: Slots 4 * q to 4 * q + 3 hold the image blocks 2 r, 2 r + 1, 2 r + 16 and 2 r + 32 / 2 + 1 for some r, each r once, so that slot_block is a permutation of the blocks. `aperture_anchor`: every aperture covers at least 8 image blocks, and at most 2 of them held by one shot index; every aperture reaches 2 for some shot index.
All inputs are finite; a program needn't handle non-finite values.
Results may differ from the reference program's by a relative error of at most 0.0003.
Values may be sent and summed in bfloat16 or wider, within the bound.
A program may use at most 64 MiB of HBM per device.

```python
import math
import jax
import jax.numpy as jnp
from jax import lax

AY = 128
NT = 8
WMAX = 4
SHOTS = 8
NB = 32
AX = 16
NZ = 32


def draw_slot_block(key, part):
    holders = NB // 4
    order = jax.random.permutation(key, holders)
    first = 2 * order
    middle = NB // 2
    blocks = jnp.stack([first, first + 1, first + middle, first + middle + 1], axis=1)
    return blocks.reshape(NB).astype(jnp.int32)


def set_ends(values, own_key, least, top_value):
    spot = [jax.random.randint(jax.random.fold_in(own_key, axis), (), 0, length) for axis, length in enumerate(values.shape)]
    longest = values.shape.index(max(values.shape))
    beside = spot[:longest] + [(spot[longest] + 1) % values.shape[longest]] + spot[longest + 1:]
    return values.at[tuple(spot)].set(least).at[tuple(beside)].set(top_value)


def steps_of(stream_key, dims, shards, smallest, largest):
    gain = 1.0
    for position, blocks in shards:
        draws = jax.random.uniform(jax.random.fold_in(jax.random.fold_in(stream_key, 6), position), (blocks,), jnp.float32, smallest / len(shards), largest / len(shards))
        gain = gain * jnp.repeat(jnp.exp(draws), dims[position] // blocks).reshape((-1,) + (1,) * (len(dims) - 1 - position))
    return gain


def gaussian(rng, shape, width, limit, split=(), held_as=jnp.bfloat16):
    array = jax.random.normal(rng, shape, jnp.float32) * width
    if len(split) > 0:
        array = steps_of(rng, shape, split, -0.22, 0.18) * array
    return jnp.clip(array, min=-limit, max=limit).astype(held_as)


def setup_inputs(seed: int = 0) -> dict:
    key_of = jax.random.split(jax.random.key(seed), 11)
    prev_fields = gaussian(key_of[0], (SHOTS, 2, NZ, AX, AY), 1.0, 6.0, ((0, 8), (2, 4)), jnp.float32)
    cur_fields = gaussian(key_of[1], (SHOTS, 2, NZ, AX, AY), 1.0, 6.0, ((0, 8), (2, 4)), jnp.float32)
    speed_term = jnp.clip(0.039794922 + 0.079833984 * jax.random.uniform(key_of[2], (SHOTS, NZ, AX, AY), jnp.float32) ** steps_of(key_of[2], (SHOTS, NZ, AX, AY), ((0, 8), (1, 4)), -0.2, 0.2), 0.039794922, 0.119628906).astype(jnp.bfloat16)
    epsilon = jnp.clip(0.25 * jax.random.uniform(key_of[3], (SHOTS, NZ, AX, AY), jnp.float32) ** steps_of(key_of[3], (SHOTS, NZ, AX, AY), ((0, 8), (1, 4)), -0.2, 0.2), 0.0, 0.25).astype(jnp.bfloat16)
    tilt = jnp.clip(1.5 * jax.random.uniform(key_of[4], (SHOTS, NZ, AX, AY), jnp.float32) ** steps_of(key_of[4], (SHOTS, NZ, AX, AY), ((0, 8), (1, 4)), -0.2, 0.2), 0.0, 1.5).astype(jnp.bfloat16)
    azimuth = jnp.clip(jax.random.uniform(key_of[5], (SHOTS, NZ, AX, AY), jnp.float32, -3.140625, 3.140625), -3.140625, 3.140625).astype(jnp.bfloat16)
    aperture_anchor = set_ends(jax.random.randint(key_of[6], (SHOTS,), 0 - AX // 2, NB - AX // 2 + 1), jax.random.fold_in(key_of[6], 1), 0 - AX // 2, (NB - AX // 2 + 1) - 1).astype(jnp.int32)
    slot_block = draw_slot_block(jax.random.fold_in(key_of[10], 71), 0)
    band_width = set_ends(jax.random.randint(key_of[8], (NZ,), 1, WMAX + 1), jax.random.fold_in(key_of[8], 1), 1, WMAX).astype(jnp.int32)
    depth_damp = jnp.clip(jnp.exp(jax.random.uniform(key_of[9], (NZ,), jnp.float32, math.log(0.02), math.log(0.1))), 0.02, 0.1)
    return {"prev_fields": prev_fields, "cur_fields": cur_fields, "speed_term": speed_term, "epsilon": epsilon, "tilt": tilt, "azimuth": azimuth, "aperture_anchor": aperture_anchor, "slot_block": slot_block, "band_width": band_width, "depth_damp": depth_damp}


def weights_of(speed_term, epsilon, tilt, azimuth):
    speed = speed_term.astype(jnp.float32)
    ratio = epsilon.astype(jnp.float32)
    theta = tilt.astype(jnp.float32)
    sweep = azimuth.astype(jnp.float32)
    sine = jnp.sin(theta)
    axis_z = jnp.cos(theta)
    axis_x = sine * jnp.cos(sweep)
    axis_y = sine * jnp.sin(sweep)
    iso_part = 1.0 + 2.0 * ratio
    anisotropy = -2.0 * ratio
    return (speed * (iso_part + anisotropy * axis_z * axis_z), speed * (iso_part + anisotropy * axis_x * axis_x), speed * (iso_part + anisotropy * axis_y * axis_y), speed * (2.0 * anisotropy * axis_z * axis_x), speed * (2.0 * anisotropy * axis_z * axis_y), speed * (2.0 * anisotropy * axis_x * axis_y))

def apply_operator(extended, weights):
    leading = extended.ndim - 3
    padded = jnp.pad(extended, [(0, 0)] * leading + [(0, 0), (1, 1), (1, 1)])
    center = padded[..., 1:-1, 1:-1, 1:-1]
    along_z = padded[..., 2:, 1:-1, 1:-1] + padded[..., :-2, 1:-1, 1:-1] - 2.0 * center
    along_x = padded[..., 1:-1, 2:, 1:-1] + padded[..., 1:-1, :-2, 1:-1] - 2.0 * center
    along_y = padded[..., 1:-1, 1:-1, 2:] + padded[..., 1:-1, 1:-1, :-2] - 2.0 * center
    cross_zx = 0.25 * (padded[..., 2:, 2:, 1:-1] - padded[..., 2:, :-2, 1:-1] - padded[..., :-2, 2:, 1:-1] + padded[..., :-2, :-2, 1:-1])
    cross_zy = 0.25 * (padded[..., 2:, 1:-1, 2:] - padded[..., 2:, 1:-1, :-2] - padded[..., :-2, 1:-1, 2:] + padded[..., :-2, 1:-1, :-2])
    cross_xy = 0.25 * (padded[..., 1:-1, 2:, 2:] - padded[..., 1:-1, 2:, :-2] - padded[..., 1:-1, :-2, 2:] + padded[..., 1:-1, :-2, :-2])
    return weights[0] * along_z + weights[1] * along_x + weights[2] * along_y + weights[3] * cross_zx + weights[4] * cross_zy + weights[5] * cross_xy

def band_matrix(band_width, depth_damp):
    length = band_width.shape[0]
    index = jnp.arange(length, dtype=jnp.int32)
    distance = jnp.abs(index[:, None] - index[None, :])
    reach = jnp.maximum(band_width[:, None], band_width[None, :])
    adjacent = ((distance > 0) & (distance <= reach)).astype(jnp.float32)
    return jnp.diag(depth_damp.astype(jnp.float32) + jnp.sum(adjacent, axis=1)) - adjacent

def reference(prev_fields, cur_fields, speed_term, epsilon, tilt, azimuth, aperture_anchor, slot_block, band_width, depth_damp):

    def one_shot(total, shot_index):
        earlier_field = prev_fields[shot_index]
        current = cur_fields[shot_index]
        weights = weights_of(speed_term[shot_index], epsilon[shot_index], tilt[shot_index], azimuth[shot_index])
        picture = jnp.zeros(current.shape[1:], jnp.float32)
        for counter in range(NT):
            extended = jnp.pad(current, ((0, 0), (1, 1), (0, 0), (0, 0)))
            following = 2.0 * current - earlier_field + apply_operator(extended, weights)
            picture = picture + following[0] * following[1]
            earlier_field, current = (current, following)
        picture = picture * (1.0 / NT)
        placed = jnp.transpose(picture, (1, 0, 2))
        start = (aperture_anchor[shot_index] + AX).astype(jnp.int32)
        window = lax.dynamic_slice_in_dim(total, start, AX, 0)
        total = lax.dynamic_update_slice_in_dim(total, window + placed, start, 0)
        return (total, None)
    total = jnp.zeros((NB + 2 * AX, NZ, AY), jnp.float32)
    total, unused = lax.scan(one_shot, total, jnp.arange(SHOTS, dtype=jnp.int32))
    image = total[AX:AX + NB]
    owned = image[slot_block]
    traces = jnp.transpose(owned, (0, 2, 1)).reshape(NB * AY, NZ)
    matrix = band_matrix(band_width, depth_damp)
    solved = jnp.linalg.solve(matrix, traces.T)
    return solved.T.reshape(NB, AY, NZ)
```

```python
import functools

import jax
import jax.numpy as jnp
from jax import lax
from jax.experimental import pallas as pl
from jax.experimental.pallas import tpu as pltpu
from jax.sharding import PartitionSpec as P

NT = 8
IMB = 4
WMAX = 4
PAD = 8
MESH = pl.DeviceIdType.MESH
SINE = (
    1.0,
    -1.0 / 6,
    1.0 / 120,
    -1.0 / 5040,
    1.0 / 362880,
    -1.0 / 39916800,
    1.0 / 6227020800,
)
COSINE = (
    1.0,
    -1.0 / 2,
    1.0 / 24,
    -1.0 / 720,
    1.0 / 40320,
    -1.0 / 3628800,
    1.0 / 479001600,
)


def series(square, terms):
    total = jnp.full_like(square, terms[-1])
    for term in terms[-2::-1]:
        total = total * square + term
    return total


def sine_cosine(angle):
    square = angle * angle
    return angle * series(square, SINE), series(square, COSINE)


def store_weights(raw, weights, layers):
    speed, ratio, theta, sweep = (raw[i, layers].astype(jnp.float32) for i in range(4))
    sine, axis_z = sine_cosine(theta)
    half_sine, half_cosine = sine_cosine(0.5 * sweep)
    axis_x = sine * (1.0 - 2.0 * half_sine * half_sine)
    axis_y = sine * (2.0 * half_sine * half_cosine)
    pull = speed * ratio
    base = speed + 2.0 * pull
    skew = -2.0 * pull
    skew_z, skew_x = skew * axis_z, skew * axis_x
    along_z = base + skew_z * axis_z
    along_x = base + skew_x * axis_x
    along_y = base + skew * axis_y * axis_y
    weights[0, layers] = 2.0 - 2.0 * (along_z + along_x + along_y)
    weights[1, layers] = along_z
    weights[2, layers] = along_x
    weights[3, layers] = along_y
    weights[4, layers] = 0.5 * (skew_z * axis_x)
    weights[5, layers] = 0.5 * (skew_z * axis_y)
    weights[6, layers] = 0.5 * (skew_x * axis_y)


def negative_inverse(matrix):
    size = matrix.shape[0]
    row_ids = lax.broadcasted_iota(jnp.int32, (size, size), 0)
    column_ids = lax.broadcasted_iota(jnp.int32, (size, size), 1)
    active = list(range(size // WMAX))
    while active:
        chosen, active = active[0::2], active[1::2]
        for inner in range(WMAX):
            pivots = [WMAX * block + inner for block in chosen]
            parts = []
            for k in pivots:
                row = matrix[k : k + 1, :]
                column = matrix[:, k : k + 1]
                inverse = 1.0 / matrix[k : k + 1, k : k + 1]
                parts.append((k, row * inverse, column, column * inverse, inverse))
            for k, row, column, scaled, inverse in parts:
                matrix = matrix - column * row
            for k, row, column, scaled, inverse in parts:
                matrix = jnp.where(row_ids == k, jnp.broadcast_to(row, matrix.shape), matrix)
            for k, row, column, scaled, inverse in parts:
                edge = jnp.where(row_ids[:, :1] == k, -inverse, scaled)
                matrix = jnp.where(column_ids == k, jnp.broadcast_to(edge, matrix.shape), matrix)
    return matrix


def band_matrix(widths, damp):
    size = widths.shape[1]
    row_ids = lax.broadcasted_iota(jnp.int32, (size, size), 0)
    column_ids = lax.broadcasted_iota(jnp.int32, (size, size), 1)
    same = row_ids == column_ids
    across = jnp.broadcast_to(widths.astype(jnp.float32), (size, size))
    down = jnp.sum(jnp.where(same, across, 0.0), axis=1, keepdims=True)
    distance = jnp.abs(row_ids - column_ids)
    reach = jnp.maximum(across, jnp.broadcast_to(down, (size, size)))
    near = jnp.where(distance.astype(jnp.float32) <= reach, 1.0, 0.0)
    adjacent = jnp.where(same, 0.0, near)
    diagonal = damp + jnp.sum(adjacent, axis=0, keepdims=True)
    return jnp.where(same, jnp.broadcast_to(diagonal, (size, size)), -adjacent)


def kernel(
    shots,
    depths,
    anchor,
    slots,
    widths,
    damp,
    prev_fields,
    cur_fields,
    speed_term,
    epsilon,
    tilt,
    azimuth,
    out,
    even,
    odd,
    raw,
    weights,
    picture,
    rows,
    parcels,
    arrived,
    packed,
    traces,
    inverse,
    local_sem,
    halo_send,
    halo_recv,
    shot_send,
    shot_recv,
    depth_send,
    depth_recv,
):
    shot = lax.axis_index("shot")
    depth = lax.axis_index("depth")
    slab = speed_term.shape[1]
    span = speed_term.shape[2]
    lanes = speed_term.shape[3]
    blocks = slots.shape[0]
    half = slab // 2
    top = 3 * slab
    inner = pl.ds(PAD, span)

    barrier = pltpu.get_barrier_semaphore()
    for o in range(1, depths):
        peer = {"depth": lax.rem(depth + o, depths)}
        pl.semaphore_signal(barrier, inc=1, device_id=peer, device_id_type=MESH)
    for o in range(1, shots):
        peer = {"shot": lax.rem(shot + o, shots)}
        pl.semaphore_signal(barrier, inc=1, device_id=peer, device_id_type=MESH)

    params = (speed_term, epsilon, tilt, azimuth)

    def source(i, first, last):
        if i < 2:
            return (cur_fields, prev_fields)[i].at[0, :, pl.ds(first, last - first)]
        return params[i - 2].at[0, pl.ds(first, last - first)]

    def target(i, first, last):
        if i < 2:
            return (even, odd)[i].at[:, pl.ds(first, last - first), inner]
        return raw.at[i - 2, pl.ds(first, last - first)]

    local = [
        pltpu.make_async_copy(source(i, 0, slab), target(i, slab, 2 * slab), local_sem.at[i])
        for i in range(6)
    ]
    for copy in local:
        copy.start()
    pl.semaphore_wait(barrier, depths + shots - 2)

    def halo(side, chunk, i):
        cut = 0 if i == 0 else 1
        if side == 0:
            first, last = ((half, slab), (cut, half))[chunk]
            place = first
            step = 1
        else:
            first, last = ((0, half), (half, slab - cut))[chunk]
            place = 2 * slab + first
            step = -1
        return pltpu.make_async_remote_copy(
            src_ref=source(i, first, last),
            dst_ref=target(i, place, place + last - first),
            send_sem=halo_send.at[side, chunk, i],
            recv_sem=halo_recv.at[side, chunk, i],
            device_id={"depth": lax.rem(depth + step + depths, depths)},
            device_id_type=MESH,
        )

    has_next = depth < depths - 1
    has_before = depth > 0
    for chunk in range(2):

        @pl.when(has_next)
        def _():
            for i in range(6):
                halo(0, chunk, i).start()

        @pl.when(has_before)
        def _():
            for i in range(6):
                halo(1, chunk, i).start()

    margin = jnp.zeros((2, top, PAD, lanes), jnp.float32)
    for field in (even, odd):
        field[:, :, 0:PAD] = margin
        field[:, :, PAD + span : 2 * PAD + span] = margin

    def clear(first):
        layers = pl.ds(first, slab)
        for field in (even, odd):
            field[:, layers, inner] = jnp.zeros((2, slab, span, lanes), jnp.float32)
        for i in range(4):
            raw[i, layers] = jnp.zeros((slab, span, lanes), raw.dtype)

    pl.when(jnp.logical_not(has_before))(lambda: clear(0))
    pl.when(jnp.logical_not(has_next))(lambda: clear(2 * slab))

    for copy in local:
        copy.wait()
    for first in range(slab, 2 * slab, 2):
        store_weights(raw, weights, pl.ds(first, 2))
    inverse[...] = negative_inverse(band_matrix(widths[...], damp[...]))
    picture[...] = jnp.zeros(picture.shape, jnp.float32)

    lane_ids = lax.broadcasted_iota(jnp.int32, (2, span, lanes), 2)
    not_first = lane_ids > 0
    not_last = lane_ids < lanes - 1

    def beside(value):
        after = jnp.where(not_last, pltpu.roll(value, lanes - 1, 2), 0.0)
        before = jnp.where(not_first, pltpu.roll(value, 1, 2), 0.0)
        return after, before

    def layer_parts(now, z, whole):
        center = now[:, z, PAD : PAD + span]
        after_x = now[:, z, PAD + 1 : PAD + 1 + span]
        before_x = now[:, z, PAD - 1 : PAD - 1 + span]
        after_y, before_y = beside(center)
        slope_x = after_x - before_x
        slope_y = after_y - before_y
        if not whole:
            return center, slope_x, slope_y
        after_xy, before_xy = beside(slope_x)
        return (
            center,
            slope_x,
            slope_y,
            after_x + before_x,
            after_y + before_y,
            after_xy - before_xy,
        )

    def advance(now, new, first, last, own):
        below = layer_parts(now, first - 1, False)
        here = layer_parts(now, first, True)
        for z in range(first, last):
            above = layer_parts(now, z + 1, z + 1 < last)
            center, _, _, sum_x, sum_y, cross_xy = here
            w = [weights[i, z][None] for i in range(7)]
            total = w[0] * center - new[:, z, PAD : PAD + span]
            total = total + w[1] * (above[0] + below[0])
            total = total + w[2] * sum_x
            total = total + w[3] * sum_y
            total = total + w[4] * (above[1] - below[1])
            total = total + w[5] * (above[2] - below[2])
            total = total + w[6] * cross_xy
            new[:, z, PAD : PAD + span] = total
            if own and slab <= z < 2 * slab:
                picture[z - slab] += total[0] * total[1]
            below, here = here, above

    def arrive(chunk):
        @pl.when(has_before)
        def _():
            for i in range(6):
                halo(0, chunk, i).wait_recv()

        @pl.when(has_next)
        def _():
            for i in range(6):
                halo(1, chunk, i).wait_recv()

    fields = (even, odd)
    arrive(0)
    for first in range(half, slab, 2):
        store_weights(raw, weights, pl.ds(first, 2))
        store_weights(raw, weights, pl.ds(2 * slab + first - half, 2))
    for t in range(1, half + 1):
        now, new = fields[(t - 1) % 2], fields[t % 2]
        advance(now, new, half + t, top - half - t, True)
    arrive(1)
    for first, count in ((1, half - 1), (top - half, half - 1)):
        store_weights(raw, weights, pl.ds(first, count))
    for t in range(1, half + 1):
        now, new = fields[(t - 1) % 2], fields[t % 2]
        advance(now, new, t, half + t, False)
        advance(now, new, top - half - t, top - t, False)
    for t in range(half + 1, NT + 1):
        now, new = fields[(t - 1) % 2], fields[t % 2]
        advance(now, new, t, top - t, True)

    rows[...] = jnp.swapaxes(picture[...], 0, 1)

    my_anchor = anchor[shot]

    def parcel(o):
        return pltpu.make_async_remote_copy(
            src_ref=parcels.at[o],
            dst_ref=arrived.at[o],
            send_sem=shot_send.at[o],
            recv_sem=shot_recv.at[o],
            device_id={"shot": lax.rem(shot + o, shots)},
            device_id_type=MESH,
        )

    for o in list(range(1, shots)) + [0]:
        holder = lax.rem(shot + o, shots)
        lowest = slots[holder * IMB]
        for j in range(1, IMB):
            lowest = jnp.minimum(lowest, slots[holder * IMB + j])
        for c in range(2):
            near = lowest + c - my_anchor
            far = near + blocks // 2
            near_in = (near >= 0) & (near < span)
            far_in = (far >= 0) & (far < span)
            index = jnp.where(near_in, near, jnp.where(far_in, far, 0))
            gain = jnp.where(near_in | far_in, 1.0 / NT, 0.0).astype(jnp.float32)
            value = rows[index] * gain
            if o == 0:
                arrived[0, c] = value
            else:
                parcels[o, c] = value
        if o > 0:
            parcel(o).start()

    owned = [jnp.zeros((slab, lanes), jnp.float32) for _ in range(IMB)]
    held = [slots[shot * IMB + j] for j in range(IMB)]
    for o in range(shots):
        if o > 0:
            parcel(o).wait_recv()
        pair = arrived[o]
        from_anchor = anchor[lax.rem(shot + shots - o, shots)]
        for j in range(IMB):
            place = held[j] - from_anchor
            inside = (place >= 0) & (place < span)
            value = jnp.where(lax.rem(held[j], 2) == 0, pair[0], pair[1])
            owned[j] = owned[j] + jnp.where(inside, value, 0.0)

    share = lanes // depths
    lane_row = lax.broadcasted_iota(jnp.int32, (slab, lanes), 1)

    def slice_for(o):
        return pltpu.make_async_remote_copy(
            src_ref=packed.at[o],
            dst_ref=traces.at[pl.ds(pl.multiple_of(depth * slab, slab), slab)],
            send_sem=depth_send.at[o],
            recv_sem=depth_recv.at[o],
            device_id={"depth": lax.rem(depth + o, depths)},
            device_id_type=MESH,
        )

    for o in list(range(1, depths)) + [0]:
        peer = lax.rem(depth + o, depths)
        block = jnp.zeros((slab, lanes), jnp.float32)
        for j in range(IMB):
            shift = lax.rem(j * share - peer * share + lanes, lanes)
            moved = pltpu.roll(owned[j], shift, 1)
            here = (lane_row >= j * share) & (lane_row < (j + 1) * share)
            block = jnp.where(here, moved, block)
        if o == 0:
            traces[pl.ds(pl.multiple_of(depth * slab, slab), slab)] = block
        else:
            packed[o] = block
            slice_for(o).start()
    for o in range(1, depths):
        slice_for(o).wait_recv()
    solved = lax.dot_general(
        traces[...],
        inverse[...],
        (((0,), (0,)), ((), ())),
        precision=lax.Precision.HIGHEST,
        preferred_element_type=jnp.float32,
    )
    out[...] = -solved[: IMB * share].reshape(out.shape)

    for chunk in range(2):

        @pl.when(has_next)
        def _():
            for i in range(6):
                halo(0, chunk, i).wait_send()

        @pl.when(has_before)
        def _():
            for i in range(6):
                halo(1, chunk, i).wait_send()

    for o in range(1, shots):
        parcel(o).wait_send()
    for o in range(1, depths):
        slice_for(o).wait_send()


def shards(
    shots,
    depths,
    prev_fields,
    cur_fields,
    speed_term,
    epsilon,
    tilt,
    azimuth,
    aperture_anchor,
    slot_block,
    band_width,
    depth_damp,
):
    slab, span, lanes = speed_term.shape[1:]
    total = band_width.shape[0]
    f32 = jnp.float32
    smem = pl.BlockSpec(memory_space=pltpu.SMEM)
    vmem = pl.BlockSpec(memory_space=pltpu.VMEM)
    anywhere = pl.BlockSpec(memory_space=pl.ANY)
    return pl.pallas_call(
        functools.partial(kernel, shots, depths),
        name="migrate",
        out_shape=jax.ShapeDtypeStruct((IMB, lanes // depths, total), f32),
        in_specs=[smem, smem, vmem, vmem] + [anywhere] * 6,
        out_specs=vmem,
        scratch_shapes=[
            pltpu.VMEM((2, 3 * slab, span + 2 * PAD, lanes), f32),
            pltpu.VMEM((2, 3 * slab, span + 2 * PAD, lanes), f32),
            pltpu.VMEM((4, 3 * slab, span, lanes), speed_term.dtype),
            pltpu.VMEM((7, 3 * slab, span, lanes), f32),
            pltpu.VMEM((slab, span, lanes), f32),
            pltpu.VMEM((span, slab, lanes), f32),
            pltpu.VMEM((shots, 2, slab, lanes), f32),
            pltpu.VMEM((shots, 2, slab, lanes), f32),
            pltpu.VMEM((depths, slab, lanes), f32),
            pltpu.VMEM((total, lanes), f32),
            pltpu.VMEM((total, total), f32),
            pltpu.SemaphoreType.DMA((6,)),
            pltpu.SemaphoreType.DMA((2, 2, 6)),
            pltpu.SemaphoreType.DMA((2, 2, 6)),
            pltpu.SemaphoreType.DMA((shots,)),
            pltpu.SemaphoreType.DMA((shots,)),
            pltpu.SemaphoreType.DMA((depths,)),
            pltpu.SemaphoreType.DMA((depths,)),
        ],
        compiler_params=pltpu.CompilerParams(
            collective_id=0, has_side_effects=True, vmem_limit_bytes=48 * 1024 * 1024
        ),
    )(
        aperture_anchor,
        slot_block,
        band_width.reshape(1, total),
        depth_damp.reshape(1, total),
        prev_fields,
        cur_fields,
        speed_term,
        epsilon,
        tilt,
        azimuth,
    )


def solution(mesh):
    placed = (
        P("shot", None, "depth", None, None),
        P("shot", None, "depth", None, None),
        P("shot", "depth", None, None),
        P("shot", "depth", None, None),
        P("shot", "depth", None, None),
        P("shot", "depth", None, None),
        P(),
        P(),
        P(),
        P(),
    )
    return jax.shard_map(
        functools.partial(shards, mesh.shape["shot"], mesh.shape["depth"]),
        mesh=mesh,
        in_specs=placed,
        out_specs=P("shot", "depth", None),
        check_vma=False,
    )
```

```python
import functools

import jax
import jax.numpy as jnp
from jax import lax
from jax.experimental import pallas as pl
from jax.experimental.pallas import tpu as pltpu
from jax.sharding import PartitionSpec as P

NT = 8
IMB = 4
WMAX = 4
PAD = 8
EARLY = 3
MESH = pl.DeviceIdType.MESH
SINE = (
    1.0,
    -1.0 / 6,
    1.0 / 120,
    -1.0 / 5040,
    1.0 / 362880,
    -1.0 / 39916800,
    1.0 / 6227020800,
)
COSINE = (
    1.0,
    -1.0 / 2,
    1.0 / 24,
    -1.0 / 720,
    1.0 / 40320,
    -1.0 / 3628800,
    1.0 / 479001600,
)


def series(square, terms):
    total = jnp.full_like(square, terms[-1])
    for term in terms[-2::-1]:
        total = total * square + term
    return total


def sine_cosine(angle):
    square = angle * angle
    return angle * series(square, SINE), series(square, COSINE)


def store_weights(raw, weights, layers):
    speed, ratio, theta, sweep = (raw[i, layers].astype(jnp.float32) for i in range(4))
    sine, axis_z = sine_cosine(theta)
    half_sine, half_cosine = sine_cosine(0.5 * sweep)
    axis_x = sine * (1.0 - 2.0 * half_sine * half_sine)
    axis_y = sine * (2.0 * half_sine * half_cosine)
    pull = speed * ratio
    base = speed + 2.0 * pull
    skew = -2.0 * pull
    skew_z, skew_x = skew * axis_z, skew * axis_x
    along_z = base + skew_z * axis_z
    along_x = base + skew_x * axis_x
    along_y = base + skew * axis_y * axis_y
    weights[0, layers] = 2.0 - 2.0 * (along_z + along_x + along_y)
    weights[1, layers] = along_z
    weights[2, layers] = along_x
    weights[3, layers] = along_y
    weights[4, layers] = 0.5 * (skew_z * axis_x)
    weights[5, layers] = 0.5 * (skew_z * axis_y)
    weights[6, layers] = 0.5 * (skew_x * axis_y)


def sweep_rounds(matrix, result):
    size = matrix.shape[0]
    row_ids = lax.broadcasted_iota(jnp.int32, (size, size), 0)
    column_ids = lax.broadcasted_iota(jnp.int32, (size, size), 1)
    active = list(range(size // WMAX))
    while active:
        chosen, active = active[0::2], active[1::2]
        for inner in range(WMAX):
            pivots = [WMAX * block + inner for block in chosen]
            parts = []
            for k in pivots:
                row = matrix[k : k + 1, :]
                column = matrix[:, k : k + 1]
                inverse = 1.0 / matrix[k : k + 1, k : k + 1]
                parts.append((k, row * inverse, column, column * inverse, inverse))
            for k, row, column, scaled, inverse in parts:
                matrix = matrix - column * row
            for k, row, column, scaled, inverse in parts:
                matrix = jnp.where(row_ids == k, jnp.broadcast_to(row, matrix.shape), matrix)
            for k, row, column, scaled, inverse in parts:
                edge = jnp.where(row_ids[:, :1] == k, -inverse, scaled)
                matrix = jnp.where(column_ids == k, jnp.broadcast_to(edge, matrix.shape), matrix)
            if inner == WMAX - 1 and not active:
                result[...] = matrix
            yield


def band_matrix(widths, damp):
    size = widths.shape[1]
    row_ids = lax.broadcasted_iota(jnp.int32, (size, size), 0)
    column_ids = lax.broadcasted_iota(jnp.int32, (size, size), 1)
    same = row_ids == column_ids
    across = jnp.broadcast_to(widths.astype(jnp.float32), (size, size))
    down = jnp.sum(jnp.where(same, across, 0.0), axis=1, keepdims=True)
    distance = jnp.abs(row_ids - column_ids)
    reach = jnp.maximum(across, jnp.broadcast_to(down, (size, size)))
    near = jnp.where(distance.astype(jnp.float32) <= reach, 1.0, 0.0)
    adjacent = jnp.where(same, 0.0, near)
    diagonal = damp + jnp.sum(adjacent, axis=0, keepdims=True)
    return jnp.where(same, jnp.broadcast_to(diagonal, (size, size)), -adjacent)


def kernel(
    shots,
    depths,
    anchor_in,
    slots_in,
    widths_in,
    damp_in,
    prev_fields,
    cur_fields,
    speed_term,
    epsilon,
    tilt,
    azimuth,
    out,
    anchor,
    slots,
    widths,
    damp,
    even,
    odd,
    raw,
    weights,
    picture,
    rows,
    parcels,
    arrived,
    packed,
    traces,
    inverse,
    local_sem,
    halo_send,
    halo_recv,
    shot_send,
    shot_recv,
    depth_send,
    depth_recv,
):
    shot = lax.axis_index("shot")
    depth = lax.axis_index("depth")
    slab = speed_term.shape[1]
    span = speed_term.shape[2]
    lanes = speed_term.shape[3]
    blocks = slots_in.shape[0]
    half = slab // 2
    top = 3 * slab
    inner = pl.ds(PAD, span)

    barrier = pltpu.get_barrier_semaphore()
    for o in range(1, depths):
        peer = {"depth": lax.rem(depth + o, depths)}
        pl.semaphore_signal(barrier, inc=1, device_id=peer, device_id_type=MESH)
    for o in range(1, shots):
        peer = {"shot": lax.rem(shot + o, shots)}
        pl.semaphore_signal(barrier, inc=1, device_id=peer, device_id_type=MESH)

    params = (speed_term, epsilon, tilt, azimuth)

    def source(i, first, last):
        if i < 2:
            return (cur_fields, prev_fields)[i].at[0, :, pl.ds(first, last - first)]
        return params[i - 2].at[0, pl.ds(first, last - first)]

    def target(i, first, last):
        if i < 2:
            return (even, odd)[i].at[:, pl.ds(first, last - first), inner]
        return raw.at[i - 2, pl.ds(first, last - first)]

    local = [
        pltpu.make_async_copy(source(i, 0, slab), target(i, slab, 2 * slab), local_sem.at[i])
        for i in range(6)
    ]
    small = ((anchor_in, anchor), (slots_in, slots), (widths_in, widths), (damp_in, damp))
    local += [
        pltpu.make_async_copy(small[i][0], small[i][1], local_sem.at[6 + i]) for i in range(4)
    ]
    for copy in local:
        copy.start()
    pl.semaphore_wait(barrier, depths + shots - 2)

    def halo(side, chunk, i):
        cut = 0 if i == 0 else 1
        if side == 0:
            first, last = ((half, slab), (cut, half))[chunk]
            place = first
            step = 1
        else:
            first, last = ((0, half), (half, slab - cut))[chunk]
            place = 2 * slab + first
            step = -1
        return pltpu.make_async_remote_copy(
            src_ref=source(i, first, last),
            dst_ref=target(i, place, place + last - first),
            send_sem=halo_send.at[side, chunk, i],
            recv_sem=halo_recv.at[side, chunk, i],
            device_id={"depth": lax.rem(depth + step + depths, depths)},
            device_id_type=MESH,
        )

    has_next = depth < depths - 1
    has_before = depth > 0
    for chunk in range(2):

        @pl.when(has_next)
        def _():
            for i in range(6):
                halo(0, chunk, i).start()

        @pl.when(has_before)
        def _():
            for i in range(6):
                halo(1, chunk, i).start()

    margin = jnp.zeros((2, top, PAD, lanes), jnp.float32)
    for field in (even, odd):
        field[:, :, 0:PAD] = margin
        field[:, :, PAD + span : 2 * PAD + span] = margin

    def clear(first):
        layers = pl.ds(first, slab)
        for field in (even, odd):
            field[:, layers, inner] = jnp.zeros((2, slab, span, lanes), jnp.float32)
        for i in range(4):
            raw[i, layers] = jnp.zeros((slab, span, lanes), raw.dtype)

    pl.when(jnp.logical_not(has_before))(lambda: clear(0))
    pl.when(jnp.logical_not(has_next))(lambda: clear(2 * slab))

    for copy in local:
        copy.wait()
    for first in range(slab, 2 * slab, 2):
        store_weights(raw, weights, pl.ds(first, 2))
    rounds = sweep_rounds(band_matrix(widths[...], damp[...]), inverse)
    for _ in range(EARLY):
        next(rounds, None)
    picture[...] = jnp.zeros(picture.shape, jnp.float32)

    lane_ids = lax.broadcasted_iota(jnp.int32, (2, span, lanes), 2)
    not_first = lane_ids > 0
    not_last = lane_ids < lanes - 1

    def beside(value):
        after = jnp.where(not_last, pltpu.roll(value, lanes - 1, 2), 0.0)
        before = jnp.where(not_first, pltpu.roll(value, 1, 2), 0.0)
        return after, before

    def layer_parts(now, z, whole):
        center = now[:, z, PAD : PAD + span]
        after_x = now[:, z, PAD + 1 : PAD + 1 + span]
        before_x = now[:, z, PAD - 1 : PAD - 1 + span]
        after_y, before_y = beside(center)
        slope_x = after_x - before_x
        slope_y = after_y - before_y
        if not whole:
            return center, slope_x, slope_y
        after_xy, before_xy = beside(slope_x)
        return (
            center,
            slope_x,
            slope_y,
            after_x + before_x,
            after_y + before_y,
            after_xy - before_xy,
        )

    def advance(now, new, first, last, own):
        below = layer_parts(now, first - 1, False)
        here = layer_parts(now, first, True)
        for z in range(first, last):
            above = layer_parts(now, z + 1, z + 1 < last)
            center, _, _, sum_x, sum_y, cross_xy = here
            w = [weights[i, z][None] for i in range(7)]
            total = w[0] * center - new[:, z, PAD : PAD + span]
            total = total + w[1] * (above[0] + below[0])
            total = total + w[2] * sum_x
            total = total + w[3] * sum_y
            total = total + w[4] * (above[1] - below[1])
            total = total + w[5] * (above[2] - below[2])
            total = total + w[6] * cross_xy
            new[:, z, PAD : PAD + span] = total
            if own and slab <= z < 2 * slab:
                picture[z - slab] += total[0] * total[1]
            below, here = here, above
        next(rounds, None)

    def arrive(chunk):
        @pl.when(has_before)
        def _():
            for i in range(6):
                halo(0, chunk, i).wait_recv()

        @pl.when(has_next)
        def _():
            for i in range(6):
                halo(1, chunk, i).wait_recv()

    fields = (even, odd)
    arrive(0)
    for first in range(half, slab, 2):
        store_weights(raw, weights, pl.ds(first, 2))
        store_weights(raw, weights, pl.ds(2 * slab + first - half, 2))
    for t in range(1, half + 1):
        now, new = fields[(t - 1) % 2], fields[t % 2]
        advance(now, new, half + t, top - half - t, True)
    arrive(1)
    for first, count in ((1, half - 1), (top - half, half - 1)):
        store_weights(raw, weights, pl.ds(first, count))
    for t in range(1, half + 1):
        now, new = fields[(t - 1) % 2], fields[t % 2]
        advance(now, new, t, half + t, False)
        advance(now, new, top - half - t, top - t, False)
    for t in range(half + 1, NT + 1):
        now, new = fields[(t - 1) % 2], fields[t % 2]
        advance(now, new, t, top - t, True)

    for _ in rounds:
        pass
    rows[...] = jnp.swapaxes(picture[...], 0, 1)

    my_anchor = anchor[shot]

    def parcel(o):
        return pltpu.make_async_remote_copy(
            src_ref=parcels.at[o],
            dst_ref=arrived.at[o],
            send_sem=shot_send.at[o],
            recv_sem=shot_recv.at[o],
            device_id={"shot": lax.rem(shot + o, shots)},
            device_id_type=MESH,
        )

    for o in list(range(1, shots)) + [0]:
        holder = lax.rem(shot + o, shots)
        lowest = slots[holder * IMB]
        for j in range(1, IMB):
            lowest = jnp.minimum(lowest, slots[holder * IMB + j])
        for c in range(2):
            near = lowest + c - my_anchor
            far = near + blocks // 2
            near_in = (near >= 0) & (near < span)
            far_in = (far >= 0) & (far < span)
            index = jnp.where(near_in, near, jnp.where(far_in, far, 0))
            gain = jnp.where(near_in | far_in, 1.0 / NT, 0.0).astype(jnp.float32)
            value = rows[index] * gain
            if o == 0:
                arrived[0, c] = value
            else:
                parcels[o, c] = value
        if o > 0:
            parcel(o).start()

    owned = [jnp.zeros((slab, lanes), jnp.float32) for _ in range(IMB)]
    held = [slots[shot * IMB + j] for j in range(IMB)]
    for o in range(shots):
        if o > 0:
            parcel(o).wait_recv()
        pair = arrived[o]
        from_anchor = anchor[lax.rem(shot + shots - o, shots)]
        for j in range(IMB):
            place = held[j] - from_anchor
            inside = (place >= 0) & (place < span)
            value = jnp.where(lax.rem(held[j], 2) == 0, pair[0], pair[1])
            owned[j] = owned[j] + jnp.where(inside, value, 0.0)

    share = lanes // depths
    lane_row = lax.broadcasted_iota(jnp.int32, (slab, lanes), 1)

    def slice_for(o):
        return pltpu.make_async_remote_copy(
            src_ref=packed.at[o],
            dst_ref=traces.at[pl.ds(pl.multiple_of(depth * slab, slab), slab)],
            send_sem=depth_send.at[o],
            recv_sem=depth_recv.at[o],
            device_id={"depth": lax.rem(depth + o, depths)},
            device_id_type=MESH,
        )

    for o in list(range(1, depths)) + [0]:
        peer = lax.rem(depth + o, depths)
        block = jnp.zeros((slab, lanes), jnp.float32)
        for j in range(IMB):
            shift = lax.rem(j * share - peer * share + lanes, lanes)
            moved = pltpu.roll(owned[j], shift, 1)
            here = (lane_row >= j * share) & (lane_row < (j + 1) * share)
            block = jnp.where(here, moved, block)
        if o == 0:
            traces[pl.ds(pl.multiple_of(depth * slab, slab), slab)] = block
        else:
            packed[o] = block
            slice_for(o).start()
    for o in range(1, depths):
        slice_for(o).wait_recv()
    solved = lax.dot_general(
        traces[...],
        inverse[...],
        (((0,), (0,)), ((), ())),
        precision=lax.Precision.HIGHEST,
        preferred_element_type=jnp.float32,
    )
    out[...] = -solved[: IMB * share].reshape(out.shape)

    for chunk in range(2):

        @pl.when(has_next)
        def _():
            for i in range(6):
                halo(0, chunk, i).wait_send()

        @pl.when(has_before)
        def _():
            for i in range(6):
                halo(1, chunk, i).wait_send()

    for o in range(1, shots):
        parcel(o).wait_send()
    for o in range(1, depths):
        slice_for(o).wait_send()


def shards(
    shots,
    depths,
    prev_fields,
    cur_fields,
    speed_term,
    epsilon,
    tilt,
    azimuth,
    aperture_anchor,
    slot_block,
    band_width,
    depth_damp,
):
    slab, span, lanes = speed_term.shape[1:]
    total = band_width.shape[0]
    f32 = jnp.float32
    vmem = pl.BlockSpec(memory_space=pltpu.VMEM)
    far = pl.BlockSpec(memory_space=pltpu.HBM)
    return pl.pallas_call(
        functools.partial(kernel, shots, depths),
        name="migrate",
        out_shape=jax.ShapeDtypeStruct((IMB, lanes // depths, total), f32),
        in_specs=[far] * 10,
        out_specs=vmem,
        scratch_shapes=[
            pltpu.SMEM(aperture_anchor.shape, jnp.int32),
            pltpu.SMEM(slot_block.shape, jnp.int32),
            pltpu.VMEM((1, total), jnp.int32),
            pltpu.VMEM((1, total), f32),
            pltpu.VMEM((2, 3 * slab, span + 2 * PAD, lanes), f32),
            pltpu.VMEM((2, 3 * slab, span + 2 * PAD, lanes), f32),
            pltpu.VMEM((4, 3 * slab, span, lanes), speed_term.dtype),
            pltpu.VMEM((7, 3 * slab, span, lanes), f32),
            pltpu.VMEM((slab, span, lanes), f32),
            pltpu.VMEM((span, slab, lanes), f32),
            pltpu.VMEM((shots, 2, slab, lanes), f32),
            pltpu.VMEM((shots, 2, slab, lanes), f32),
            pltpu.VMEM((depths, slab, lanes), f32),
            pltpu.VMEM((total, lanes), f32),
            pltpu.VMEM((total, total), f32),
            pltpu.SemaphoreType.DMA((10,)),
            pltpu.SemaphoreType.DMA((2, 2, 6)),
            pltpu.SemaphoreType.DMA((2, 2, 6)),
            pltpu.SemaphoreType.DMA((shots,)),
            pltpu.SemaphoreType.DMA((shots,)),
            pltpu.SemaphoreType.DMA((depths,)),
            pltpu.SemaphoreType.DMA((depths,)),
        ],
        compiler_params=pltpu.CompilerParams(
            collective_id=0, has_side_effects=True, vmem_limit_bytes=64 * 1024 * 1024
        ),
    )(
        aperture_anchor,
        slot_block,
        band_width.reshape(1, total),
        depth_damp.reshape(1, total),
        prev_fields,
        cur_fields,
        speed_term,
        epsilon,
        tilt,
        azimuth,
    )


def solution(mesh):
    placed = (
        P("shot", None, "depth", None, None),
        P("shot", None, "depth", None, None),
        P("shot", "depth", None, None),
        P("shot", "depth", None, None),
        P("shot", "depth", None, None),
        P("shot", "depth", None, None),
        P(),
        P(),
        P(),
        P(),
    )
    return jax.shard_map(
        functools.partial(shards, mesh.shape["shot"], mesh.shape["depth"]),
        mesh=mesh,
        in_specs=placed,
        out_specs=P("shot", "depth", None),
        check_vma=False,
    )
```

```python
import functools

import jax
import jax.numpy as jnp
from jax import lax
from jax.experimental import pallas as pl
from jax.experimental.pallas import tpu as pltpu
from jax.sharding import PartitionSpec as P

NT = 8
IMB = 4
WMAX = 4
PAD = 8
EARLY = 3
MESH = pl.DeviceIdType.MESH
SINE = (
    1.0,
    -1.0 / 6,
    1.0 / 120,
    -1.0 / 5040,
    1.0 / 362880,
    -1.0 / 39916800,
    1.0 / 6227020800,
)
COSINE = (
    1.0,
    -1.0 / 2,
    1.0 / 24,
    -1.0 / 720,
    1.0 / 40320,
    -1.0 / 3628800,
    1.0 / 479001600,
)


def series(square, terms):
    total = jnp.full_like(square, terms[-1])
    for term in terms[-2::-1]:
        total = total * square + term
    return total


def sine_cosine(angle):
    square = angle * angle
    return angle * series(square, SINE), series(square, COSINE)


def store_weights(raw, weights, layers):
    speed, ratio, theta, sweep = (raw[i, layers].astype(jnp.float32) for i in range(4))
    sine, axis_z = sine_cosine(theta)
    half_sine, half_cosine = sine_cosine(0.5 * sweep)
    axis_x = sine * (1.0 - 2.0 * half_sine * half_sine)
    axis_y = sine * (2.0 * half_sine * half_cosine)
    pull = speed * ratio
    base = speed + 2.0 * pull
    skew = -2.0 * pull
    skew_z, skew_x = skew * axis_z, skew * axis_x
    along_z = base + skew_z * axis_z
    along_x = base + skew_x * axis_x
    along_y = base + skew * axis_y * axis_y
    weights[0, layers] = 2.0 - 2.0 * (along_z + along_x + along_y)
    weights[1, layers] = along_z
    weights[2, layers] = along_x
    weights[3, layers] = along_y
    weights[4, layers] = 0.5 * (skew_z * axis_x)
    weights[5, layers] = 0.5 * (skew_z * axis_y)
    weights[6, layers] = 0.5 * (skew_x * axis_y)


def sweep_rounds(matrix, result):
    size = matrix.shape[0]
    row_ids = lax.broadcasted_iota(jnp.int32, (size, size), 0)
    column_ids = lax.broadcasted_iota(jnp.int32, (size, size), 1)
    active = list(range(size // WMAX))
    while active:
        chosen, active = active[0::2], active[1::2]
        for inner in range(WMAX):
            pivots = [WMAX * block + inner for block in chosen]
            parts = []
            for k in pivots:
                row = matrix[k : k + 1, :]
                column = matrix[:, k : k + 1]
                inverse = 1.0 / matrix[k : k + 1, k : k + 1]
                parts.append((k, row * inverse, column, column * inverse, inverse))
            for k, row, column, scaled, inverse in parts:
                matrix = matrix - column * row
            for k, row, column, scaled, inverse in parts:
                matrix = jnp.where(row_ids == k, jnp.broadcast_to(row, matrix.shape), matrix)
            for k, row, column, scaled, inverse in parts:
                edge = jnp.where(row_ids[:, :1] == k, -inverse, scaled)
                matrix = jnp.where(column_ids == k, jnp.broadcast_to(edge, matrix.shape), matrix)
            if inner == WMAX - 1 and not active:
                result[...] = matrix
            yield


def band_matrix(widths, damp):
    size = widths.shape[1]
    row_ids = lax.broadcasted_iota(jnp.int32, (size, size), 0)
    column_ids = lax.broadcasted_iota(jnp.int32, (size, size), 1)
    same = row_ids == column_ids
    across = jnp.broadcast_to(widths.astype(jnp.float32), (size, size))
    down = jnp.sum(jnp.where(same, across, 0.0), axis=1, keepdims=True)
    distance = jnp.abs(row_ids - column_ids)
    reach = jnp.maximum(across, jnp.broadcast_to(down, (size, size)))
    near = jnp.where(distance.astype(jnp.float32) <= reach, 1.0, 0.0)
    adjacent = jnp.where(same, 0.0, near)
    diagonal = damp + jnp.sum(adjacent, axis=0, keepdims=True)
    return jnp.where(same, jnp.broadcast_to(diagonal, (size, size)), -adjacent)


def kernel(
    shots,
    depths,
    anchor_in,
    slots_in,
    widths_in,
    damp_in,
    prev_fields,
    cur_fields,
    speed_term,
    epsilon,
    tilt,
    azimuth,
    out,
    anchor,
    slots,
    widths,
    damp,
    even,
    odd,
    raw,
    weights,
    picture,
    rows,
    parcels,
    arrived,
    packed,
    traces,
    inverse,
    local_sem,
    halo_send,
    halo_recv,
    shot_send,
    shot_recv,
    depth_send,
    depth_recv,
):
    shot = lax.axis_index("shot")
    depth = lax.axis_index("depth")
    slab = speed_term.shape[1]
    span = speed_term.shape[2]
    lanes = speed_term.shape[3]
    blocks = slots_in.shape[0]
    half = slab // 2
    top = 3 * slab
    inner = pl.ds(PAD, span)

    barrier = pltpu.get_barrier_semaphore()
    for o in range(1, depths):
        peer = {"depth": lax.rem(depth + o, depths)}
        pl.semaphore_signal(barrier, inc=1, device_id=peer, device_id_type=MESH)
    for o in range(1, shots):
        peer = {"shot": lax.rem(shot + o, shots)}
        pl.semaphore_signal(barrier, inc=1, device_id=peer, device_id_type=MESH)

    params = (speed_term, epsilon, tilt, azimuth)

    def source(i, first, last):
        if i < 2:
            return (cur_fields, prev_fields)[i].at[0, :, pl.ds(first, last - first)]
        return params[i - 2].at[0, pl.ds(first, last - first)]

    def target(i, first, last):
        if i < 2:
            return (even, odd)[i].at[:, pl.ds(first, last - first), inner]
        return raw.at[i - 2, pl.ds(first, last - first)]

    local = [
        pltpu.make_async_copy(source(i, 0, slab), target(i, slab, 2 * slab), local_sem.at[i])
        for i in range(6)
    ]
    small = ((anchor_in, anchor), (slots_in, slots), (widths_in, widths), (damp_in, damp))
    local += [
        pltpu.make_async_copy(small[i][0], small[i][1], local_sem.at[6 + i]) for i in range(4)
    ]
    for copy in local:
        copy.start()
    pl.semaphore_wait(barrier, depths + shots - 2)

    def halo(side, chunk, i):
        cut = 0 if i == 0 else 1
        if side == 0:
            first, last = ((half, slab), (cut, half))[chunk]
            place = first
            step = 1
        else:
            first, last = ((0, half), (half, slab - cut))[chunk]
            place = 2 * slab + first
            step = -1
        return pltpu.make_async_remote_copy(
            src_ref=source(i, first, last),
            dst_ref=target(i, place, place + last - first),
            send_sem=halo_send.at[side, chunk, i],
            recv_sem=halo_recv.at[side, chunk, i],
            device_id={"depth": lax.rem(depth + step + depths, depths)},
            device_id_type=MESH,
        )

    has_next = depth < depths - 1
    has_before = depth > 0
    for chunk in range(2):

        @pl.when(has_next)
        def _():
            for i in range(6):
                halo(0, chunk, i).start()

        @pl.when(has_before)
        def _():
            for i in range(6):
                halo(1, chunk, i).start()

    margin = jnp.zeros((2, top, PAD, lanes), jnp.float32)
    for field in (even, odd):
        field[:, :, 0:PAD] = margin
        field[:, :, PAD + span : 2 * PAD + span] = margin

    def clear(first):
        layers = pl.ds(first, slab)
        for field in (even, odd):
            field[:, layers, inner] = jnp.zeros((2, slab, span, lanes), jnp.float32)
        for i in range(4):
            raw[i, layers] = jnp.zeros((slab, span, lanes), raw.dtype)

    pl.when(jnp.logical_not(has_before))(lambda: clear(0))
    pl.when(jnp.logical_not(has_next))(lambda: clear(2 * slab))

    for copy in local:
        copy.wait()
    for first in range(slab, 2 * slab, 2):
        store_weights(raw, weights, pl.ds(first, 2))
    rounds = sweep_rounds(band_matrix(widths[...], damp[...]), inverse)
    for _ in range(EARLY):
        next(rounds, None)
    picture[...] = jnp.zeros(picture.shape, jnp.float32)

    lane_ids = lax.broadcasted_iota(jnp.int32, (2, span, lanes), 2)
    not_first = lane_ids > 0
    not_last = lane_ids < lanes - 1

    def beside(value):
        after = jnp.where(not_last, pltpu.roll(value, lanes - 1, 2), 0.0)
        before = jnp.where(not_first, pltpu.roll(value, 1, 2), 0.0)
        return after, before

    def layer_parts(now, z, whole):
        center = now[:, z, PAD : PAD + span]
        after_x = now[:, z, PAD + 1 : PAD + 1 + span]
        before_x = now[:, z, PAD - 1 : PAD - 1 + span]
        after_y, before_y = beside(center)
        slope_x = after_x - before_x
        slope_y = after_y - before_y
        if not whole:
            return center, slope_x, slope_y
        after_xy, before_xy = beside(slope_x)
        return (
            center,
            slope_x,
            slope_y,
            after_x + before_x,
            after_y + before_y,
            after_xy - before_xy,
        )

    def advance(now, new, first, last, own):
        below = layer_parts(now, first - 1, False)
        here = layer_parts(now, first, True)
        for z in range(first, last):
            above = layer_parts(now, z + 1, z + 1 < last)
            center, _, _, sum_x, sum_y, cross_xy = here
            w = [weights[i, z][None] for i in range(7)]
            total = w[0] * center - new[:, z, PAD : PAD + span]
            total = total + w[1] * (above[0] + below[0])
            total = total + w[2] * sum_x
            total = total + w[3] * sum_y
            total = total + w[4] * (above[1] - below[1])
            total = total + w[5] * (above[2] - below[2])
            total = total + w[6] * cross_xy
            new[:, z, PAD : PAD + span] = total
            if own and slab <= z < 2 * slab:
                picture[z - slab] += total[0] * total[1]
            below, here = here, above
        next(rounds, None)

    def arrive(chunk):
        @pl.when(has_before)
        def _():
            for i in range(6):
                halo(0, chunk, i).wait_recv()

        @pl.when(has_next)
        def _():
            for i in range(6):
                halo(1, chunk, i).wait_recv()

    fields = (even, odd)
    for t in range(1, half):
        now, new = fields[(t - 1) % 2], fields[t % 2]
        advance(now, new, slab + t, 2 * slab - t, True)
    arrive(0)
    for first in range(half, slab, 2):
        store_weights(raw, weights, pl.ds(first, 2))
        store_weights(raw, weights, pl.ds(2 * slab + first - half, 2))
    for t in range(1, half + 1):
        now, new = fields[(t - 1) % 2], fields[t % 2]
        advance(now, new, half + t, slab + t, True)
        advance(now, new, 2 * slab - t, top - half - t, True)
    arrive(1)
    for first, count in ((1, half - 1), (top - half, half - 1)):
        store_weights(raw, weights, pl.ds(first, count))
    for t in range(1, half + 1):
        now, new = fields[(t - 1) % 2], fields[t % 2]
        advance(now, new, t, half + t, False)
        advance(now, new, top - half - t, top - t, False)
    for t in range(half + 1, NT + 1):
        now, new = fields[(t - 1) % 2], fields[t % 2]
        advance(now, new, t, top - t, True)

    for _ in rounds:
        pass
    rows[...] = jnp.swapaxes(picture[...], 0, 1)

    my_anchor = anchor[shot]

    def parcel(o):
        return pltpu.make_async_remote_copy(
            src_ref=parcels.at[o],
            dst_ref=arrived.at[o],
            send_sem=shot_send.at[o],
            recv_sem=shot_recv.at[o],
            device_id={"shot": lax.rem(shot + o, shots)},
            device_id_type=MESH,
        )

    for o in list(range(1, shots)) + [0]:
        holder = lax.rem(shot + o, shots)
        lowest = slots[holder * IMB]
        for j in range(1, IMB):
            lowest = jnp.minimum(lowest, slots[holder * IMB + j])
        for c in range(2):
            near = lowest + c - my_anchor
            far = near + blocks // 2
            near_in = (near >= 0) & (near < span)
            far_in = (far >= 0) & (far < span)
            index = jnp.where(near_in, near, jnp.where(far_in, far, 0))
            gain = jnp.where(near_in | far_in, 1.0 / NT, 0.0).astype(jnp.float32)
            value = rows[index] * gain
            if o == 0:
                arrived[0, c] = value
            else:
                parcels[o, c] = value
        if o > 0:
            parcel(o).start()

    owned = [jnp.zeros((slab, lanes), jnp.float32) for _ in range(IMB)]
    held = [slots[shot * IMB + j] for j in range(IMB)]
    for o in range(shots):
        if o > 0:
            parcel(o).wait_recv()
        pair = arrived[o]
        from_anchor = anchor[lax.rem(shot + shots - o, shots)]
        for j in range(IMB):
            place = held[j] - from_anchor
            inside = (place >= 0) & (place < span)
            value = jnp.where(lax.rem(held[j], 2) == 0, pair[0], pair[1])
            owned[j] = owned[j] + jnp.where(inside, value, 0.0)

    share = lanes // depths
    lane_row = lax.broadcasted_iota(jnp.int32, (slab, lanes), 1)

    def slice_for(o):
        return pltpu.make_async_remote_copy(
            src_ref=packed.at[o],
            dst_ref=traces.at[pl.ds(pl.multiple_of(depth * slab, slab), slab)],
            send_sem=depth_send.at[o],
            recv_sem=depth_recv.at[o],
            device_id={"depth": lax.rem(depth + o, depths)},
            device_id_type=MESH,
        )

    for o in list(range(1, depths)) + [0]:
        peer = lax.rem(depth + o, depths)
        block = jnp.zeros((slab, lanes), jnp.float32)
        for j in range(IMB):
            shift = lax.rem(j * share - peer * share + lanes, lanes)
            moved = pltpu.roll(owned[j], shift, 1)
            here = (lane_row >= j * share) & (lane_row < (j + 1) * share)
            block = jnp.where(here, moved, block)
        if o == 0:
            traces[pl.ds(pl.multiple_of(depth * slab, slab), slab)] = block
        else:
            packed[o] = block
            slice_for(o).start()
    for o in range(1, depths):
        slice_for(o).wait_recv()
    out[...] = -jnp.dot(
        inverse[...],
        traces[...],
        precision=lax.Precision.HIGHEST,
        preferred_element_type=jnp.float32,
    )

    for chunk in range(2):

        @pl.when(has_next)
        def _():
            for i in range(6):
                halo(0, chunk, i).wait_send()

        @pl.when(has_before)
        def _():
            for i in range(6):
                halo(1, chunk, i).wait_send()

    for o in range(1, shots):
        parcel(o).wait_send()
    for o in range(1, depths):
        slice_for(o).wait_send()


def shards(
    shots,
    depths,
    prev_fields,
    cur_fields,
    speed_term,
    epsilon,
    tilt,
    azimuth,
    aperture_anchor,
    slot_block,
    band_width,
    depth_damp,
):
    slab, span, lanes = speed_term.shape[1:]
    total = band_width.shape[0]
    f32 = jnp.float32
    vmem = pl.BlockSpec(memory_space=pltpu.VMEM)
    far = pl.BlockSpec(memory_space=pltpu.HBM)
    solved = pl.pallas_call(
        functools.partial(kernel, shots, depths),
        name="migrate",
        out_shape=jax.ShapeDtypeStruct((total, lanes), f32),
        in_specs=[far] * 10,
        out_specs=vmem,
        scratch_shapes=[
            pltpu.SMEM(aperture_anchor.shape, jnp.int32),
            pltpu.SMEM(slot_block.shape, jnp.int32),
            pltpu.VMEM((1, total), jnp.int32),
            pltpu.VMEM((1, total), f32),
            pltpu.VMEM((2, 3 * slab, span + 2 * PAD, lanes), f32),
            pltpu.VMEM((2, 3 * slab, span + 2 * PAD, lanes), f32),
            pltpu.VMEM((4, 3 * slab, span, lanes), speed_term.dtype),
            pltpu.VMEM((7, 3 * slab, span, lanes), f32),
            pltpu.VMEM((slab, span, lanes), f32),
            pltpu.VMEM((span, slab, lanes), f32),
            pltpu.VMEM((shots, 2, slab, lanes), f32),
            pltpu.VMEM((shots, 2, slab, lanes), f32),
            pltpu.VMEM((depths, slab, lanes), f32),
            pltpu.VMEM((total, lanes), f32),
            pltpu.VMEM((total, total), f32),
            pltpu.SemaphoreType.DMA((10,)),
            pltpu.SemaphoreType.DMA((2, 2, 6)),
            pltpu.SemaphoreType.DMA((2, 2, 6)),
            pltpu.SemaphoreType.DMA((shots,)),
            pltpu.SemaphoreType.DMA((shots,)),
            pltpu.SemaphoreType.DMA((depths,)),
            pltpu.SemaphoreType.DMA((depths,)),
        ],
        compiler_params=pltpu.CompilerParams(
            collective_id=0, has_side_effects=True, vmem_limit_bytes=64 * 1024 * 1024
        ),
    )(
        aperture_anchor,
        slot_block,
        band_width.reshape(1, total),
        depth_damp.reshape(1, total),
        prev_fields,
        cur_fields,
        speed_term,
        epsilon,
        tilt,
        azimuth,
    )
    share = lanes // depths
    return solved[:, : IMB * share].T.reshape(IMB, share, total)


def solution(mesh):
    placed = (
        P("shot", None, "depth", None, None),
        P("shot", None, "depth", None, None),
        P("shot", "depth", None, None),
        P("shot", "depth", None, None),
        P("shot", "depth", None, None),
        P("shot", "depth", None, None),
        P(),
        P(),
        P(),
        P(),
    )
    return jax.shard_map(
        functools.partial(shards, mesh.shape["shot"], mesh.shape["depth"]),
        mesh=mesh,
        in_specs=placed,
        out_specs=P("shot", "depth", None),
        check_vma=False,
    )
```

```python
import functools

import jax
import jax.numpy as jnp
from jax import lax
from jax.experimental import pallas as pl
from jax.experimental.pallas import tpu as pltpu
from jax.sharding import PartitionSpec as P

NT = 8
IMB = 4
WMAX = 4
PAD = 8
EARLY = 3
MESH = pl.DeviceIdType.MESH
SINE = (
    1.0,
    -1.0 / 6,
    1.0 / 120,
    -1.0 / 5040,
    1.0 / 362880,
    -1.0 / 39916800,
    1.0 / 6227020800,
)
COSINE = (
    1.0,
    -1.0 / 2,
    1.0 / 24,
    -1.0 / 720,
    1.0 / 40320,
    -1.0 / 3628800,
    1.0 / 479001600,
)


def series(square, terms):
    total = jnp.full_like(square, terms[-1])
    for term in terms[-2::-1]:
        total = total * square + term
    return total


def sine_cosine(angle):
    square = angle * angle
    return angle * series(square, SINE), series(square, COSINE)


def store_weights(raw, weights, layers):
    speed, ratio, theta, sweep = (raw[i, layers].astype(jnp.float32) for i in range(4))
    sine, axis_z = sine_cosine(theta)
    half_sine, half_cosine = sine_cosine(0.5 * sweep)
    axis_x = sine * (1.0 - 2.0 * half_sine * half_sine)
    axis_y = sine * (2.0 * half_sine * half_cosine)
    pull = speed * ratio
    base = speed + 2.0 * pull
    skew = -2.0 * pull
    skew_z, skew_x = skew * axis_z, skew * axis_x
    along_z = base + skew_z * axis_z
    along_x = base + skew_x * axis_x
    along_y = base + skew * axis_y * axis_y
    weights[0, layers] = 2.0 - 2.0 * (along_z + along_x + along_y)
    weights[1, layers] = along_z
    weights[2, layers] = along_x
    weights[3, layers] = along_y
    weights[4, layers] = 0.5 * (skew_z * axis_x)
    weights[5, layers] = 0.5 * (skew_z * axis_y)
    weights[6, layers] = 0.5 * (skew_x * axis_y)


def sweep_rounds(matrix, result):
    size = matrix.shape[0]
    row_ids = lax.broadcasted_iota(jnp.int32, (size, size), 0)
    column_ids = lax.broadcasted_iota(jnp.int32, (size, size), 1)
    active = list(range(size // WMAX))
    while active:
        chosen, active = active[0::2], active[1::2]
        for inner in range(WMAX):
            pivots = [WMAX * block + inner for block in chosen]
            parts = []
            for k in pivots:
                row = matrix[k : k + 1, :]
                column = matrix[:, k : k + 1]
                inverse = 1.0 / matrix[k : k + 1, k : k + 1]
                parts.append((k, row * inverse, column, column * inverse, inverse))
            for k, row, column, scaled, inverse in parts:
                matrix = matrix - column * row
            for k, row, column, scaled, inverse in parts:
                matrix = jnp.where(row_ids == k, jnp.broadcast_to(row, matrix.shape), matrix)
            for k, row, column, scaled, inverse in parts:
                edge = jnp.where(row_ids[:, :1] == k, -inverse, scaled)
                matrix = jnp.where(column_ids == k, jnp.broadcast_to(edge, matrix.shape), matrix)
            if inner == WMAX - 1 and not active:
                result[...] = matrix
            yield


def band_matrix(widths, damp):
    size = widths.shape[1]
    row_ids = lax.broadcasted_iota(jnp.int32, (size, size), 0)
    column_ids = lax.broadcasted_iota(jnp.int32, (size, size), 1)
    same = row_ids == column_ids
    across = jnp.broadcast_to(widths.astype(jnp.float32), (size, size))
    down = jnp.sum(jnp.where(same, across, 0.0), axis=1, keepdims=True)
    distance = jnp.abs(row_ids - column_ids)
    reach = jnp.maximum(across, jnp.broadcast_to(down, (size, size)))
    near = jnp.where(distance.astype(jnp.float32) <= reach, 1.0, 0.0)
    adjacent = jnp.where(same, 0.0, near)
    diagonal = damp + jnp.sum(adjacent, axis=0, keepdims=True)
    return jnp.where(same, jnp.broadcast_to(diagonal, (size, size)), -adjacent)


def kernel(
    shots,
    depths,
    anchor_in,
    slots_in,
    widths_in,
    damp_in,
    prev_fields,
    cur_fields,
    speed_term,
    epsilon,
    tilt,
    azimuth,
    out,
    anchor,
    slots,
    widths,
    damp,
    state,
    stage,
    raw,
    weights,
    picture,
    rows,
    parcels,
    arrived,
    packed,
    traces,
    inverse,
    local_sem,
    halo_send,
    halo_recv,
    shot_send,
    shot_recv,
    depth_send,
    depth_recv,
):
    shot = lax.axis_index("shot")
    depth = lax.axis_index("depth")
    slab = speed_term.shape[1]
    span = speed_term.shape[2]
    lanes = speed_term.shape[3]
    blocks = slots_in.shape[0]
    half = slab // 2
    top = 3 * slab
    inner = pl.ds(PAD, span)
    even, odd = state.at[0], state.at[1]

    barrier = pltpu.get_barrier_semaphore()
    for o in range(1, depths):
        peer = {"depth": lax.rem(depth + o, depths)}
        pl.semaphore_signal(barrier, inc=1, device_id=peer, device_id_type=MESH)
    for o in range(1, shots):
        peer = {"shot": lax.rem(shot + o, shots)}
        pl.semaphore_signal(barrier, inc=1, device_id=peer, device_id_type=MESH)

    params = (speed_term, epsilon, tilt, azimuth)

    own = pl.ds(slab, slab)
    moves = [(cur_fields.at[0], stage.at[0]), (prev_fields.at[0], stage.at[1])]
    moves += [(params[i].at[0], raw.at[i, own]) for i in range(4)]
    moves += [(cur_fields.at[0], even.at[:, own, inner]), (prev_fields.at[0], odd.at[:, own, inner])]
    moves += [(anchor_in, anchor), (slots_in, slots), (widths_in, widths), (damp_in, damp)]
    local = [
        pltpu.make_async_copy(first, second, local_sem.at[i])
        for i, (first, second) in enumerate(moves)
    ]
    for copy in local:
        copy.start()
    pl.semaphore_wait(barrier, depths + shots - 2)
    for copy in local[:6]:
        copy.wait()

    def halo(side, chunk, i):
        cut = i
        if side == 0:
            first, last = ((half, slab), (cut, half))[chunk]
            place = first
            step = 1
        else:
            first, last = ((0, half), (half, slab - cut))[chunk]
            place = 2 * slab + first
            step = -1
        count = last - first
        if i == 0:
            here = stage.at[:, :, pl.ds(first, count)]
            there = state.at[:, :, pl.ds(place, count), inner]
        else:
            here = raw.at[:, pl.ds(slab + first, count)]
            there = raw.at[:, pl.ds(place, count)]
        return pltpu.make_async_remote_copy(
            src_ref=here,
            dst_ref=there,
            send_sem=halo_send.at[side, chunk, i],
            recv_sem=halo_recv.at[side, chunk, i],
            device_id={"depth": lax.rem(depth + step + depths, depths)},
            device_id_type=MESH,
        )

    has_next = depth < depths - 1
    has_before = depth > 0
    for chunk in range(2):

        @pl.when(has_next)
        def _():
            for i in range(2):
                halo(0, chunk, i).start()

        @pl.when(has_before)
        def _():
            for i in range(2):
                halo(1, chunk, i).start()

    margin = jnp.zeros((2, top, PAD, lanes), jnp.float32)
    for field in (even, odd):
        field[:, :, 0:PAD] = margin
        field[:, :, PAD + span : 2 * PAD + span] = margin

    def clear(first):
        layers = pl.ds(first, slab)
        for field in (even, odd):
            field[:, layers, inner] = jnp.zeros((2, slab, span, lanes), jnp.float32)
        for i in range(4):
            raw[i, layers] = jnp.zeros((slab, span, lanes), raw.dtype)

    pl.when(jnp.logical_not(has_before))(lambda: clear(0))
    pl.when(jnp.logical_not(has_next))(lambda: clear(2 * slab))

    for copy in local[6:]:
        copy.wait()
    for first in range(slab, 2 * slab, 2):
        store_weights(raw, weights, pl.ds(first, 2))
    rounds = sweep_rounds(band_matrix(widths[...], damp[...]), inverse)
    for _ in range(EARLY):
        next(rounds, None)
    picture[...] = jnp.zeros(picture.shape, jnp.float32)

    lane_ids = lax.broadcasted_iota(jnp.int32, (2, span, lanes), 2)
    not_first = lane_ids > 0
    not_last = lane_ids < lanes - 1

    def beside(value):
        after = jnp.where(not_last, pltpu.roll(value, lanes - 1, 2), 0.0)
        before = jnp.where(not_first, pltpu.roll(value, 1, 2), 0.0)
        return after, before

    def layer_parts(now, z, whole):
        center = now[:, z, PAD : PAD + span]
        after_x = now[:, z, PAD + 1 : PAD + 1 + span]
        before_x = now[:, z, PAD - 1 : PAD - 1 + span]
        after_y, before_y = beside(center)
        slope_x = after_x - before_x
        slope_y = after_y - before_y
        if not whole:
            return center, slope_x, slope_y
        after_xy, before_xy = beside(slope_x)
        return (
            center,
            slope_x,
            slope_y,
            after_x + before_x,
            after_y + before_y,
            after_xy - before_xy,
        )

    def advance(now, new, first, last, own):
        below = layer_parts(now, first - 1, False)
        here = layer_parts(now, first, True)
        for z in range(first, last):
            above = layer_parts(now, z + 1, z + 1 < last)
            center, _, _, sum_x, sum_y, cross_xy = here
            w = [weights[i, z][None] for i in range(7)]
            total = w[0] * center - new[:, z, PAD : PAD + span]
            total = total + w[1] * (above[0] + below[0])
            total = total + w[2] * sum_x
            total = total + w[3] * sum_y
            total = total + w[4] * (above[1] - below[1])
            total = total + w[5] * (above[2] - below[2])
            total = total + w[6] * cross_xy
            new[:, z, PAD : PAD + span] = total
            if own and slab <= z < 2 * slab:
                picture[z - slab] += total[0] * total[1]
            below, here = here, above
        next(rounds, None)

    def arrive(chunk):
        @pl.when(has_before)
        def _():
            for i in range(2):
                halo(0, chunk, i).wait_recv()

        @pl.when(has_next)
        def _():
            for i in range(2):
                halo(1, chunk, i).wait_recv()

    fields = (even, odd)
    for t in range(1, half):
        now, new = fields[(t - 1) % 2], fields[t % 2]
        advance(now, new, slab + t, 2 * slab - t, True)
    arrive(0)
    for first in range(half, slab, 2):
        store_weights(raw, weights, pl.ds(first, 2))
        store_weights(raw, weights, pl.ds(2 * slab + first - half, 2))
    for t in range(1, half + 1):
        now, new = fields[(t - 1) % 2], fields[t % 2]
        advance(now, new, half + t, slab + t, True)
        advance(now, new, 2 * slab - t, top - half - t, True)
    arrive(1)
    for first, count in ((1, half - 1), (top - half, half - 1)):
        store_weights(raw, weights, pl.ds(first, count))
    for t in range(1, half + 1):
        now, new = fields[(t - 1) % 2], fields[t % 2]
        advance(now, new, t, half + t, False)
        advance(now, new, top - half - t, top - t, False)
    for t in range(half + 1, NT + 1):
        now, new = fields[(t - 1) % 2], fields[t % 2]
        advance(now, new, t, top - t, True)

    for _ in rounds:
        pass
    rows[...] = jnp.swapaxes(picture[...], 0, 1)

    my_anchor = anchor[shot]

    def parcel(o):
        return pltpu.make_async_remote_copy(
            src_ref=parcels.at[o],
            dst_ref=arrived.at[o],
            send_sem=shot_send.at[o],
            recv_sem=shot_recv.at[o],
            device_id={"shot": lax.rem(shot + o, shots)},
            device_id_type=MESH,
        )

    for o in list(range(1, shots)) + [0]:
        holder = lax.rem(shot + o, shots)
        lowest = slots[holder * IMB]
        for j in range(1, IMB):
            lowest = jnp.minimum(lowest, slots[holder * IMB + j])
        for c in range(2):
            near = lowest + c - my_anchor
            far = near + blocks // 2
            near_in = (near >= 0) & (near < span)
            far_in = (far >= 0) & (far < span)
            index = jnp.where(near_in, near, jnp.where(far_in, far, 0))
            gain = jnp.where(near_in | far_in, 1.0 / NT, 0.0).astype(jnp.float32)
            value = rows[index] * gain
            if o == 0:
                arrived[0, c] = value
            else:
                parcels[o, c] = value
        if o > 0:
            parcel(o).start()

    owned = [jnp.zeros((slab, lanes), jnp.float32) for _ in range(IMB)]
    held = [slots[shot * IMB + j] for j in range(IMB)]
    for o in range(shots):
        if o > 0:
            parcel(o).wait_recv()
        pair = arrived[o]
        from_anchor = anchor[lax.rem(shot + shots - o, shots)]
        for j in range(IMB):
            place = held[j] - from_anchor
            inside = (place >= 0) & (place < span)
            value = jnp.where(lax.rem(held[j], 2) == 0, pair[0], pair[1])
            owned[j] = owned[j] + jnp.where(inside, value, 0.0)

    share = lanes // depths
    lane_row = lax.broadcasted_iota(jnp.int32, (slab, lanes), 1)

    def slice_for(o):
        return pltpu.make_async_remote_copy(
            src_ref=packed.at[o],
            dst_ref=traces.at[pl.ds(pl.multiple_of(depth * slab, slab), slab)],
            send_sem=depth_send.at[o],
            recv_sem=depth_recv.at[o],
            device_id={"depth": lax.rem(depth + o, depths)},
            device_id_type=MESH,
        )

    for o in list(range(1, depths)) + [0]:
        peer = lax.rem(depth + o, depths)
        block = jnp.zeros((slab, lanes), jnp.float32)
        for j in range(IMB):
            shift = lax.rem(j * share - peer * share + lanes, lanes)
            moved = pltpu.roll(owned[j], shift, 1)
            here = (lane_row >= j * share) & (lane_row < (j + 1) * share)
            block = jnp.where(here, moved, block)
        if o == 0:
            traces[pl.ds(pl.multiple_of(depth * slab, slab), slab)] = block
        else:
            packed[o] = block
            slice_for(o).start()
    for o in range(1, depths):
        slice_for(o).wait_recv()
    out[...] = -jnp.dot(
        inverse[...],
        traces[...],
        precision=lax.Precision.HIGHEST,
        preferred_element_type=jnp.float32,
    )

    for chunk in range(2):

        @pl.when(has_next)
        def _():
            for i in range(2):
                halo(0, chunk, i).wait_send()

        @pl.when(has_before)
        def _():
            for i in range(2):
                halo(1, chunk, i).wait_send()

    for o in range(1, shots):
        parcel(o).wait_send()
    for o in range(1, depths):
        slice_for(o).wait_send()


def shards(
    shots,
    depths,
    prev_fields,
    cur_fields,
    speed_term,
    epsilon,
    tilt,
    azimuth,
    aperture_anchor,
    slot_block,
    band_width,
    depth_damp,
):
    slab, span, lanes = speed_term.shape[1:]
    total = band_width.shape[0]
    f32 = jnp.float32
    vmem = pl.BlockSpec(memory_space=pltpu.VMEM)
    far = pl.BlockSpec(memory_space=pltpu.HBM)
    solved = pl.pallas_call(
        functools.partial(kernel, shots, depths),
        name="migrate",
        out_shape=jax.ShapeDtypeStruct((total, lanes), f32),
        in_specs=[far] * 10,
        out_specs=vmem,
        scratch_shapes=[
            pltpu.SMEM(aperture_anchor.shape, jnp.int32),
            pltpu.SMEM(slot_block.shape, jnp.int32),
            pltpu.VMEM((1, total), jnp.int32),
            pltpu.VMEM((1, total), f32),
            pltpu.VMEM((2, 2, 3 * slab, span + 2 * PAD, lanes), f32),
            pltpu.VMEM((2, 2, slab, span, lanes), f32),
            pltpu.VMEM((4, 3 * slab, span, lanes), speed_term.dtype),
            pltpu.VMEM((7, 3 * slab, span, lanes), f32),
            pltpu.VMEM((slab, span, lanes), f32),
            pltpu.VMEM((span, slab, lanes), f32),
            pltpu.VMEM((shots, 2, slab, lanes), f32),
            pltpu.VMEM((shots, 2, slab, lanes), f32),
            pltpu.VMEM((depths, slab, lanes), f32),
            pltpu.VMEM((total, lanes), f32),
            pltpu.VMEM((total, total), f32),
            pltpu.SemaphoreType.DMA((12,)),
            pltpu.SemaphoreType.DMA((2, 2, 2)),
            pltpu.SemaphoreType.DMA((2, 2, 2)),
            pltpu.SemaphoreType.DMA((shots,)),
            pltpu.SemaphoreType.DMA((shots,)),
            pltpu.SemaphoreType.DMA((depths,)),
            pltpu.SemaphoreType.DMA((depths,)),
        ],
        compiler_params=pltpu.CompilerParams(
            collective_id=0, has_side_effects=True, vmem_limit_bytes=64 * 1024 * 1024
        ),
    )(
        aperture_anchor,
        slot_block,
        band_width.reshape(1, total),
        depth_damp.reshape(1, total),
        prev_fields,
        cur_fields,
        speed_term,
        epsilon,
        tilt,
        azimuth,
    )
    share = lanes // depths
    return solved[:, : IMB * share].T.reshape(IMB, share, total)


def solution(mesh):
    placed = (
        P("shot", None, "depth", None, None),
        P("shot", None, "depth", None, None),
        P("shot", "depth", None, None),
        P("shot", "depth", None, None),
        P("shot", "depth", None, None),
        P("shot", "depth", None, None),
        P(),
        P(),
        P(),
        P(),
    )
    return jax.shard_map(
        functools.partial(shards, mesh.shape["shot"], mesh.shape["depth"]),
        mesh=mesh,
        in_specs=placed,
        out_specs=P("shot", "depth", None),
        check_vma=False,
    )
```

```python
import functools

import jax
import jax.numpy as jnp
from jax import lax
from jax.experimental import pallas as pl
from jax.experimental.pallas import tpu as pltpu
from jax.sharding import PartitionSpec as P

NT = 8
IMB = 4
WMAX = 4
PAD = 8
EARLY = 8
LATER = 5
MESH = pl.DeviceIdType.MESH
SINE = (
    1.0,
    -1.0 / 6,
    1.0 / 120,
    -1.0 / 5040,
    1.0 / 362880,
    -1.0 / 39916800,
    1.0 / 6227020800,
)
COSINE = (
    1.0,
    -1.0 / 2,
    1.0 / 24,
    -1.0 / 720,
    1.0 / 40320,
    -1.0 / 3628800,
    1.0 / 479001600,
)


def series(square, terms):
    total = jnp.full_like(square, terms[-1])
    for term in terms[-2::-1]:
        total = total * square + term
    return total


def sine_cosine(angle):
    square = angle * angle
    return angle * series(square, SINE), series(square, COSINE)


def store_weights(raw, weights, layers):
    speed, ratio, theta, sweep = (raw[i, layers].astype(jnp.float32) for i in range(4))
    sine, axis_z = sine_cosine(theta)
    half_sine, half_cosine = sine_cosine(0.5 * sweep)
    axis_x = sine * (1.0 - 2.0 * half_sine * half_sine)
    axis_y = sine * (2.0 * half_sine * half_cosine)
    pull = speed * ratio
    base = speed + 2.0 * pull
    skew = -2.0 * pull
    skew_z, skew_x = skew * axis_z, skew * axis_x
    along_z = base + skew_z * axis_z
    along_x = base + skew_x * axis_x
    along_y = base + skew * axis_y * axis_y
    weights[0, layers] = 2.0 - 2.0 * (along_z + along_x + along_y)
    weights[1, layers] = along_z
    weights[2, layers] = along_x
    weights[3, layers] = along_y
    weights[4, layers] = 0.5 * (skew_z * axis_x)
    weights[5, layers] = 0.5 * (skew_z * axis_y)
    weights[6, layers] = 0.5 * (skew_x * axis_y)


def sweep_rounds(matrix, result):
    size = matrix.shape[0]
    row_ids = lax.broadcasted_iota(jnp.int32, (size, size), 0)
    column_ids = lax.broadcasted_iota(jnp.int32, (size, size), 1)
    active = list(range(size // WMAX))
    while active:
        chosen, active = active[0::2], active[1::2]
        for inner in range(WMAX):
            pivots = [WMAX * block + inner for block in chosen]
            parts = []
            for k in pivots:
                row = matrix[k : k + 1, :]
                column = matrix[:, k : k + 1]
                inverse = 1.0 / matrix[k : k + 1, k : k + 1]
                parts.append((k, row * inverse, column, column * inverse, inverse))
            for k, row, column, scaled, inverse in parts:
                matrix = matrix - column * row
            for k, row, column, scaled, inverse in parts:
                matrix = jnp.where(row_ids == k, jnp.broadcast_to(row, matrix.shape), matrix)
            for k, row, column, scaled, inverse in parts:
                edge = jnp.where(row_ids[:, :1] == k, -inverse, scaled)
                matrix = jnp.where(column_ids == k, jnp.broadcast_to(edge, matrix.shape), matrix)
            if inner == WMAX - 1 and not active:
                result[...] = matrix
            yield


def band_matrix(widths, damp):
    size = widths.shape[1]
    row_ids = lax.broadcasted_iota(jnp.int32, (size, size), 0)
    column_ids = lax.broadcasted_iota(jnp.int32, (size, size), 1)
    same = row_ids == column_ids
    across = jnp.broadcast_to(widths.astype(jnp.float32), (size, size))
    down = jnp.sum(jnp.where(same, across, 0.0), axis=1, keepdims=True)
    distance = jnp.abs(row_ids - column_ids)
    reach = jnp.maximum(across, jnp.broadcast_to(down, (size, size)))
    near = jnp.where(distance.astype(jnp.float32) <= reach, 1.0, 0.0)
    adjacent = jnp.where(same, 0.0, near)
    diagonal = damp + jnp.sum(adjacent, axis=0, keepdims=True)
    return jnp.where(same, jnp.broadcast_to(diagonal, (size, size)), -adjacent)


def kernel(
    shots,
    depths,
    anchor_in,
    slots_in,
    widths_in,
    damp_in,
    prev_fields,
    cur_fields,
    speed_term,
    epsilon,
    tilt,
    azimuth,
    out,
    anchor,
    slots,
    widths,
    damp,
    state,
    stage,
    raw,
    weights,
    picture,
    rows,
    parcels,
    arrived,
    packed,
    traces,
    inverse,
    local_sem,
    halo_send,
    halo_recv,
    shot_send,
    shot_recv,
    depth_send,
    depth_recv,
):
    shot = lax.axis_index("shot")
    depth = lax.axis_index("depth")
    slab = speed_term.shape[1]
    span = speed_term.shape[2]
    lanes = speed_term.shape[3]
    blocks = slots_in.shape[0]
    half = slab // 2
    top = 3 * slab
    inner = pl.ds(PAD, span)
    even, odd = state.at[0], state.at[1]

    barrier = pltpu.get_barrier_semaphore()
    for o in range(1, depths):
        peer = {"depth": lax.rem(depth + o, depths)}
        pl.semaphore_signal(barrier, inc=1, device_id=peer, device_id_type=MESH)
    for o in range(1, shots):
        peer = {"shot": lax.rem(shot + o, shots)}
        pl.semaphore_signal(barrier, inc=1, device_id=peer, device_id_type=MESH)

    params = (speed_term, epsilon, tilt, azimuth)

    own = pl.ds(slab, slab)
    moves = [(cur_fields.at[0], stage.at[0]), (prev_fields.at[0], stage.at[1])]
    moves += [(params[i].at[0], raw.at[i, own]) for i in range(4)]
    moves += [(cur_fields.at[0], even.at[:, own, inner]), (prev_fields.at[0], odd.at[:, own, inner])]
    moves += [(anchor_in, anchor), (slots_in, slots), (widths_in, widths), (damp_in, damp)]
    local = [
        pltpu.make_async_copy(first, second, local_sem.at[i])
        for i, (first, second) in enumerate(moves)
    ]
    for copy in local:
        copy.start()
    pl.semaphore_wait(barrier, depths + shots - 2)
    for copy in local[:6]:
        copy.wait()

    def halo(side, chunk, i):
        cut = i
        if side == 0:
            first, last = ((half, slab), (cut, half))[chunk]
            place = first
            step = 1
        else:
            first, last = ((0, half), (half, slab - cut))[chunk]
            place = 2 * slab + first
            step = -1
        count = last - first
        if i == 0:
            here = stage.at[:, :, pl.ds(first, count)]
            there = state.at[:, :, pl.ds(place, count), inner]
        else:
            here = raw.at[:, pl.ds(slab + first, count)]
            there = raw.at[:, pl.ds(place, count)]
        return pltpu.make_async_remote_copy(
            src_ref=here,
            dst_ref=there,
            send_sem=halo_send.at[side, chunk, i],
            recv_sem=halo_recv.at[side, chunk, i],
            device_id={"depth": lax.rem(depth + step + depths, depths)},
            device_id_type=MESH,
        )

    has_next = depth < depths - 1
    has_before = depth > 0
    for chunk in range(2):

        @pl.when(has_next)
        def _():
            for i in range(2):
                halo(0, chunk, i).start()

        @pl.when(has_before)
        def _():
            for i in range(2):
                halo(1, chunk, i).start()

    margin = jnp.zeros((2, top, PAD, lanes), jnp.float32)
    for field in (even, odd):
        field[:, :, 0:PAD] = margin
        field[:, :, PAD + span : 2 * PAD + span] = margin

    def clear(first):
        layers = pl.ds(first, slab)
        for field in (even, odd):
            field[:, layers, inner] = jnp.zeros((2, slab, span, lanes), jnp.float32)
        for i in range(4):
            raw[i, layers] = jnp.zeros((slab, span, lanes), raw.dtype)

    pl.when(jnp.logical_not(has_before))(lambda: clear(0))
    pl.when(jnp.logical_not(has_next))(lambda: clear(2 * slab))

    for copy in local[6:]:
        copy.wait()
    for first in range(slab, 2 * slab, 2):
        store_weights(raw, weights, pl.ds(first, 2))
    rounds = sweep_rounds(band_matrix(widths[...], damp[...]), inverse)
    for _ in range(EARLY):
        next(rounds, None)
    picture[...] = jnp.zeros(picture.shape, jnp.float32)

    lane_ids = lax.broadcasted_iota(jnp.int32, (2, span, lanes), 2)
    not_first = lane_ids > 0
    not_last = lane_ids < lanes - 1

    def beside(value):
        after = jnp.where(not_last, pltpu.roll(value, lanes - 1, 2), 0.0)
        before = jnp.where(not_first, pltpu.roll(value, 1, 2), 0.0)
        return after, before

    def layer_parts(now, z, whole):
        center = now[:, z, PAD : PAD + span]
        after_x = now[:, z, PAD + 1 : PAD + 1 + span]
        before_x = now[:, z, PAD - 1 : PAD - 1 + span]
        after_y, before_y = beside(center)
        slope_x = after_x - before_x
        slope_y = after_y - before_y
        if not whole:
            return center, slope_x, slope_y
        after_xy, before_xy = beside(slope_x)
        return (
            center,
            slope_x,
            slope_y,
            after_x + before_x,
            after_y + before_y,
            after_xy - before_xy,
        )

    def advance(now, new, first, last, own):
        below = layer_parts(now, first - 1, False)
        here = layer_parts(now, first, True)
        for z in range(first, last):
            above = layer_parts(now, z + 1, z + 1 < last)
            center, _, _, sum_x, sum_y, cross_xy = here
            w = [weights[i, z][None] for i in range(7)]
            total = w[0] * center - new[:, z, PAD : PAD + span]
            total = total + w[1] * (above[0] + below[0])
            total = total + w[2] * sum_x
            total = total + w[3] * sum_y
            total = total + w[4] * (above[1] - below[1])
            total = total + w[5] * (above[2] - below[2])
            total = total + w[6] * cross_xy
            new[:, z, PAD : PAD + span] = total
            if own and slab <= z < 2 * slab:
                picture[z - slab] += total[0] * total[1]
            below, here = here, above

    def arrive(chunk):
        @pl.when(has_before)
        def _():
            for i in range(2):
                halo(0, chunk, i).wait_recv()

        @pl.when(has_next)
        def _():
            for i in range(2):
                halo(1, chunk, i).wait_recv()

    fields = (even, odd)
    for t in range(1, half):
        now, new = fields[(t - 1) % 2], fields[t % 2]
        advance(now, new, slab + t, 2 * slab - t, True)
    arrive(0)
    for first in range(half, slab, 2):
        store_weights(raw, weights, pl.ds(first, 2))
        store_weights(raw, weights, pl.ds(2 * slab + first - half, 2))
    for t in range(1, half + 1):
        now, new = fields[(t - 1) % 2], fields[t % 2]
        advance(now, new, half + t, slab + t, True)
        advance(now, new, 2 * slab - t, top - half - t, True)
    arrive(1)
    for first, count in ((1, half - 1), (top - half, half - 1)):
        store_weights(raw, weights, pl.ds(first, count))
    for t in range(1, half + 1):
        now, new = fields[(t - 1) % 2], fields[t % 2]
        advance(now, new, t, half + t, False)
        advance(now, new, top - half - t, top - t, False)
    for t in range(half + 1, NT + 1):
        now, new = fields[(t - 1) % 2], fields[t % 2]
        advance(now, new, t, top - t, True)

    rows[...] = jnp.swapaxes(picture[...], 0, 1)

    my_anchor = anchor[shot]

    def parcel(o):
        return pltpu.make_async_remote_copy(
            src_ref=parcels.at[o],
            dst_ref=arrived.at[o],
            send_sem=shot_send.at[o],
            recv_sem=shot_recv.at[o],
            device_id={"shot": lax.rem(shot + o, shots)},
            device_id_type=MESH,
        )

    for o in list(range(1, shots)) + [0]:
        holder = lax.rem(shot + o, shots)
        lowest = slots[holder * IMB]
        for j in range(1, IMB):
            lowest = jnp.minimum(lowest, slots[holder * IMB + j])
        for c in range(2):
            near = lowest + c - my_anchor
            far = near + blocks // 2
            near_in = (near >= 0) & (near < span)
            far_in = (far >= 0) & (far < span)
            index = jnp.where(near_in, near, jnp.where(far_in, far, 0))
            gain = jnp.where(near_in | far_in, 1.0 / NT, 0.0).astype(jnp.float32)
            value = rows[index] * gain
            if o == 0:
                arrived[0, c] = value
            else:
                parcels[o, c] = value
        if o > 0:
            parcel(o).start()

    for _ in range(LATER):
        next(rounds, None)
    owned = [jnp.zeros((slab, lanes), jnp.float32) for _ in range(IMB)]
    held = [slots[shot * IMB + j] for j in range(IMB)]
    for o in range(shots):
        if o > 0:
            parcel(o).wait_recv()
        pair = arrived[o]
        from_anchor = anchor[lax.rem(shot + shots - o, shots)]
        for j in range(IMB):
            place = held[j] - from_anchor
            inside = (place >= 0) & (place < span)
            value = jnp.where(lax.rem(held[j], 2) == 0, pair[0], pair[1])
            owned[j] = owned[j] + jnp.where(inside, value, 0.0)

    share = lanes // depths
    lane_row = lax.broadcasted_iota(jnp.int32, (slab, lanes), 1)

    def slice_for(o):
        return pltpu.make_async_remote_copy(
            src_ref=packed.at[o],
            dst_ref=traces.at[pl.ds(pl.multiple_of(depth * slab, slab), slab)],
            send_sem=depth_send.at[o],
            recv_sem=depth_recv.at[o],
            device_id={"depth": lax.rem(depth + o, depths)},
            device_id_type=MESH,
        )

    for o in list(range(1, depths)) + [0]:
        peer = lax.rem(depth + o, depths)
        block = jnp.zeros((slab, lanes), jnp.float32)
        for j in range(IMB):
            shift = lax.rem(j * share - peer * share + lanes, lanes)
            moved = pltpu.roll(owned[j], shift, 1)
            here = (lane_row >= j * share) & (lane_row < (j + 1) * share)
            block = jnp.where(here, moved, block)
        if o == 0:
            traces[pl.ds(pl.multiple_of(depth * slab, slab), slab)] = block
        else:
            packed[o] = block
            slice_for(o).start()
    for _ in rounds:
        pass
    for o in range(1, depths):
        slice_for(o).wait_recv()
    out[...] = -jnp.dot(
        inverse[...],
        traces[...],
        precision=lax.Precision.HIGHEST,
        preferred_element_type=jnp.float32,
    )

    for chunk in range(2):

        @pl.when(has_next)
        def _():
            for i in range(2):
                halo(0, chunk, i).wait_send()

        @pl.when(has_before)
        def _():
            for i in range(2):
                halo(1, chunk, i).wait_send()

    for o in range(1, shots):
        parcel(o).wait_send()
    for o in range(1, depths):
        slice_for(o).wait_send()


def shards(
    shots,
    depths,
    prev_fields,
    cur_fields,
    speed_term,
    epsilon,
    tilt,
    azimuth,
    aperture_anchor,
    slot_block,
    band_width,
    depth_damp,
):
    slab, span, lanes = speed_term.shape[1:]
    total = band_width.shape[0]
    f32 = jnp.float32
    vmem = pl.BlockSpec(memory_space=pltpu.VMEM)
    far = pl.BlockSpec(memory_space=pltpu.HBM)
    solved = pl.pallas_call(
        functools.partial(kernel, shots, depths),
        name="migrate",
        out_shape=jax.ShapeDtypeStruct((total, lanes), f32),
        in_specs=[far] * 10,
        out_specs=vmem,
        scratch_shapes=[
            pltpu.SMEM(aperture_anchor.shape, jnp.int32),
            pltpu.SMEM(slot_block.shape, jnp.int32),
            pltpu.VMEM((1, total), jnp.int32),
            pltpu.VMEM((1, total), f32),
            pltpu.VMEM((2, 2, 3 * slab, span + 2 * PAD, lanes), f32),
            pltpu.VMEM((2, 2, slab, span, lanes), f32),
            pltpu.VMEM((4, 3 * slab, span, lanes), speed_term.dtype),
            pltpu.VMEM((7, 3 * slab, span, lanes), f32),
            pltpu.VMEM((slab, span, lanes), f32),
            pltpu.VMEM((span, slab, lanes), f32),
            pltpu.VMEM((shots, 2, slab, lanes), f32),
            pltpu.VMEM((shots, 2, slab, lanes), f32),
            pltpu.VMEM((depths, slab, lanes), f32),
            pltpu.VMEM((total, lanes), f32),
            pltpu.VMEM((total, total), f32),
            pltpu.SemaphoreType.DMA((12,)),
            pltpu.SemaphoreType.DMA((2, 2, 2)),
            pltpu.SemaphoreType.DMA((2, 2, 2)),
            pltpu.SemaphoreType.DMA((shots,)),
            pltpu.SemaphoreType.DMA((shots,)),
            pltpu.SemaphoreType.DMA((depths,)),
            pltpu.SemaphoreType.DMA((depths,)),
        ],
        compiler_params=pltpu.CompilerParams(
            collective_id=0, has_side_effects=True, vmem_limit_bytes=64 * 1024 * 1024
        ),
    )(
        aperture_anchor,
        slot_block,
        band_width.reshape(1, total),
        depth_damp.reshape(1, total),
        prev_fields,
        cur_fields,
        speed_term,
        epsilon,
        tilt,
        azimuth,
    )
    share = lanes // depths
    return solved[:, : IMB * share].T.reshape(IMB, share, total)


def solution(mesh):
    placed = (
        P("shot", None, "depth", None, None),
        P("shot", None, "depth", None, None),
        P("shot", "depth", None, None),
        P("shot", "depth", None, None),
        P("shot", "depth", None, None),
        P("shot", "depth", None, None),
        P(),
        P(),
        P(),
        P(),
    )
    return jax.shard_map(
        functools.partial(shards, mesh.shape["shot"], mesh.shape["depth"]),
        mesh=mesh,
        in_specs=placed,
        out_specs=P("shot", "depth", None),
        check_vma=False,
    )
```
